768 devices in a mesh: row: 24 (over z, y_hi), col: 32 (over y_lo, x, core).
Axes of the slice: x: 4, y: 8 (y_hi: 2, y_lo: 4; y = y_hi * 4 + y_lo), z: 12, core: 2. Of those that a mesh axis runs over, the one named last changes fastest.
Arguments:
- vectors: float32 [786432, 256], P(('row', 'col')), may hold values from -6 to 6
- blocks: float32 [6144, 5, 128, 128], P(('row', 'col')), may hold values from -0.25 to 0.25
- pattern: int32 [6144, 5], P(('row', 'col')), may hold values from 0 to 6143, as said below
- counts: int32 [6144], P(('row', 'col')), may hold values from 1 to 5, as said below
Outputs:
- filtered: float32 [786432, 256], P(('row', 'col'))
The draws below stay inside these ranges and needn't reach their ends.
Inputs may be any that keep to these rules, and one draw needn't show every extreme that they name: `pattern`: block row a = ((r * 32 + c) * 2 + u) * 4 + v is the site (r * 2 + u, c * 4 + v) of a periodic lattice of 48 x 128 sites; its 5 slots name, in an order that varies from row to row, the block rows of that site and of the four sites one step away along either lattice direction, with wrap-around. The live slots of a block row are its first counts ones; some block row holds exactly 5 live slots and some exactly 1.
All inputs are finite; a program needn't handle non-finite values.
Results may differ from the reference program's by a relative error of at most 0.000084.
Values sent between devices are 32-bit elements; how exact they have to be, the bound alone decides.
A program may use at most 64 MiB of HBM per device.

```python
import jax
import jax.numpy as jnp
from jax import lax

BS = 128
W = 256
SLOTS = 5
TY = 2
TX = 4
BR = 8
NB = 6144
ORDER = 786432
N_ROW = 24
N_COL = 32


def draw_pattern(key, part):
    key = jax.random.fold_in(key, 11)
    block_ids = jnp.arange(NB, dtype=jnp.int32)
    site_x = block_ids % TX
    site_y = block_ids // TX % TY
    owner = block_ids // (TX * TY)
    lat_y = owner // N_COL * TY + site_y
    lat_x = owner % N_COL * TX + site_x
    scores = jax.random.randint(key, (NB, SLOTS), 0, 1048576) * SLOTS + jnp.arange(SLOTS, dtype=jnp.int32)[None, :]
    order = jnp.argsort(scores, axis=1).astype(jnp.int32)
    step_y = jnp.array([0, 0, 0, -1, 1], dtype=jnp.int32)[order]
    step_x = jnp.array([0, -1, 1, 0, 0], dtype=jnp.int32)[order]
    target_y = jnp.remainder(lat_y[:, None] + step_y, TY * N_ROW)
    target_x = jnp.remainder(lat_x[:, None] + step_x, TX * N_COL)
    target_owner = target_y // TY * N_COL + target_x // TX
    result = (target_owner * TY + target_y % TY) * TX + target_x % TX
    return result.astype(jnp.int32)


def draw_counts(key, part):
    key = jax.random.fold_in(key, 23)
    key_level, key_extra = jax.random.split(key)
    level = jax.random.randint(key_level, (NB // BR,), 0, 4)
    extra = jax.random.randint(key_extra, (NB,), 0, 2)
    owner = jnp.arange(NB, dtype=jnp.int32) // BR
    values = jnp.clip(1 + 2 * level[owner] - extra, 1, SLOTS)
    values = values.at[0].set(SLOTS)
    values = values.at[1].set(1)
    return values.astype(jnp.int32)


def block_levels(key, extent, shards, smallest, largest):
    factor_of, own = 1.0, jax.random.fold_in(key, 6)
    for dim, blocks in shards:
        heights = jnp.exp(jax.random.uniform(jax.random.fold_in(own, dim), (blocks,), jnp.float32, smallest / len(shards), largest / len(shards)))
        factor_of = factor_of * jnp.repeat(heights, extent[dim] // blocks).reshape([-1 if axis == dim else 1 for axis in range(len(extent))])
    return factor_of


def centred(stream_key, dims, spread, most, cuts=(), held_as=jnp.bfloat16):
    loudness = block_levels(stream_key, dims, cuts, -0.22, 0.18) if cuts else 1.0
    entries = jax.random.normal(stream_key, dims, jnp.float32) * spread * loudness
    return jnp.minimum(jnp.maximum(entries, -most), most).astype(held_as)


def setup_inputs(seed: int = 0) -> dict:
    keys = jax.random.split(jax.random.key(seed), 5)
    return {
        "vectors": centred(keys[0], (ORDER, W), 1.0, 6.0, ((0, 768),), jnp.float32),
        "blocks": centred(keys[1], (NB, SLOTS, BS, BS), (SLOTS * BS) ** -0.5, 0.25, ((0, 768),), jnp.float32),
        "pattern": draw_pattern(jax.random.fold_in(keys[4], 71), 0),
        "counts": draw_counts(jax.random.fold_in(keys[4], 71), 0),
    }


center_shift = 0.25
half_range = 1.0


def apply_hamiltonian(field, blocks, pattern, counts):
    field_blocks = field.reshape(NB, BS, W)
    live = (jnp.arange(SLOTS, dtype=jnp.int32)[None, :] < counts[:, None]).astype(jnp.float32)
    group_count = NB // BR
    grouped_blocks = blocks.reshape(group_count, BR, SLOTS, BS, BS)
    grouped_pattern = pattern.reshape(group_count, BR, SLOTS)
    grouped_live = live.reshape(group_count, BR, SLOTS)

    def one_group(items):
        group_blocks, group_pattern, group_live = items
        columns = field_blocks[group_pattern]
        masked = group_blocks * group_live[:, :, None, None]
        return jnp.einsum("bsij,bsjw->biw", masked, columns, precision=lax.Precision.HIGHEST, preferred_element_type=jnp.float32)

    result = lax.map(one_group, (grouped_blocks, grouped_pattern, grouped_live))
    return result.reshape(ORDER, W)


def reference(vectors, blocks, pattern, counts):
    first = (apply_hamiltonian(vectors, blocks, pattern, counts) - center_shift * vectors) / half_range
    second = apply_hamiltonian(first, blocks, pattern, counts)
    return (2.0 / half_range) * (second - center_shift * first) - vectors
```

```python
import functools

import jax
import jax.numpy as jnp
from jax import lax
from jax.experimental import pallas as pl
from jax.experimental.pallas import tpu as pltpu
from jax.sharding import PartitionSpec as P

TY = 2
MESH = pl.DeviceIdType.MESH

center_shift = 0.25
half_range = 1.0

OWN, INNER, LEFT, RIGHT, OUTER = range(5)


def dot(a, b):
    return jnp.dot(a, b, precision=lax.Precision.HIGHEST, preferred_element_type=jnp.float32)


def kernel(
    rows, cols, tx,
    vec_hbm, blk_hbm, pattern, counts, out_hbm,
    vec, blk, amat, first, out, halo_row, halo_col,
    load_sem, store_sem, row_send, row_recv, col_send, col_recv,
):
    bs = vec.shape[1]
    slots = blk.shape[1]
    sites = TY * tx
    me_r, me_c = lax.axis_index("row"), lax.axis_index("col")
    row_of = (lax.rem(me_r + rows - 1, rows), lax.rem(me_r + 1, rows))
    col_of = (lax.rem(me_c + cols - 1, cols), lax.rem(me_c + 1, cols))
    row_dev = [(r, me_c) for r in row_of]
    col_dev = [(me_r, c) for c in col_of]

    load_blk = pltpu.make_async_copy(blk_hbm, blk, load_sem.at[0])
    load_vec = pltpu.make_async_copy(vec_hbm, vec, load_sem.at[1])
    load_vec.start()
    load_blk.start()

    barrier = pltpu.get_barrier_semaphore()
    for device in row_dev + col_dev:
        pl.semaphore_signal(barrier, inc=1, device_id=device, device_id_type=MESH)
    pl.semaphore_wait(barrier, 4)

    def row_copy(source, step, u, v):
        return pltpu.make_async_remote_copy(
            src_ref=source.at[u * tx + v], dst_ref=halo_row.at[step, 1 - u, v],
            send_sem=row_send.at[step, 1 - u, v], recv_sem=row_recv.at[step, 1 - u, v],
            device_id=row_dev[u], device_id_type=MESH,
        )

    def col_copy(source, step, side, u):
        v = 0 if side == 0 else tx - 1
        return pltpu.make_async_remote_copy(
            src_ref=source.at[u * tx + v], dst_ref=halo_col.at[step, 1 - side, u],
            send_sem=col_send.at[step, 1 - side, u], recv_sem=col_recv.at[step, 1 - side, u],
            device_id=col_dev[side], device_id_type=MESH,
        )

    edges = [0, tx - 1]
    inside = list(range(1, tx - 1))
    for u in range(TY):
        for side in range(2):
            col_copy(vec_hbm, 0, side, u).start()
    for v in edges + inside:
        for u in range(TY):
            row_copy(vec_hbm, 0, u, v).start()

    def site_id(y, x):
        return ((y // TY * cols + x // tx) * TY + y % TY) * tx + x % tx

    load_blk.wait()
    for u in range(TY):
        for v in range(tx):
            a = u * tx + v
            y, x = me_r * TY + u, me_c * tx + v
            up = lax.rem(y + TY * rows - 1, TY * rows)
            down = lax.rem(y + 1, TY * rows)
            left = lax.rem(x + tx * cols - 1, tx * cols)
            right = lax.rem(x + 1, tx * cols)
            target = [(y, x), (down if u == 0 else up, x), (y, left), (y, right), (up if u == 0 else down, x)]
            for d in range(5):
                name = site_id(*target[d])
                slot = jnp.int32(0)
                for s in range(1, slots):
                    slot = jnp.where(pattern[a, s] == name, s, slot)
                live = jnp.where(slot < counts[a], 1.0, 0.0)
                amat[a, :, d * bs:(d + 1) * bs] = blk[a, slot] * live

    load_vec.wait()

    def partial(field, step, u, v):
        a = u * tx + v
        near = [
            field[a],
            field[(1 - u) * tx + v],
            halo_col[step, 0, u] if v == 0 else field[a - 1],
            halo_col[step, 1, u] if v == tx - 1 else field[a + 1],
        ]
        total = dot(amat[a, :, :2 * bs], jnp.concatenate(near[:2], axis=0))
        total += dot(amat[a, :, 2 * bs:4 * bs], jnp.concatenate(near[2:], axis=0))
        return total - center_shift * near[0]

    def outer(step, u, v):
        return dot(amat[u * tx + v, :, 4 * bs:], halo_row[step, u, v])

    for step, field, result in ((0, vec, first), (1, first, out)):
        for v in inside:
            for u in range(TY):
                result[u * tx + v] = partial(field, step, u, v)
        for u in range(TY):
            for side in range(2):
                col_copy(field, step, side, u).wait_recv()
        for v in edges:
            for u in range(TY):
                result[u * tx + v] = partial(field, step, u, v)
        for v in edges + inside:
            for u in range(TY):
                a = u * tx + v
                row_copy(field, step, 1 - u, v).wait_recv()
                total = (result[a] + outer(step, u, v)) / half_range
                if step == 0:
                    first[a] = total
                    row_copy(first, 1, u, v).start()
                    if v == 0:
                        col_copy(first, 1, 0, u).start()
                    if v == tx - 1:
                        col_copy(first, 1, 1, u).start()
                else:
                    out[a] = 2.0 * total - vec[a]
                    pltpu.make_async_copy(out.at[a], out_hbm.at[a], store_sem.at[a]).start()

    for a in range(sites):
        pltpu.make_async_copy(out.at[a], out_hbm.at[a], store_sem.at[a]).wait()
    for step, field in ((0, vec_hbm), (1, first)):
        for u in range(TY):
            for v in range(tx):
                row_copy(field, step, u, v).wait_send()
            for side in range(2):
                col_copy(field, step, side, u).wait_send()


def body(vectors, blocks, pattern, counts):
    local, slots, bs, _ = blocks.shape
    width = vectors.shape[1]
    rows, cols = lax.axis_size("row"), lax.axis_size("col")
    tx = local // TY
    f32 = jnp.float32
    anywhere = pl.BlockSpec(memory_space=pl.ANY)
    scalars = pl.BlockSpec(memory_space=pltpu.SMEM)
    dma = pltpu.SemaphoreType.DMA
    result = pl.pallas_call(
        functools.partial(kernel, rows, cols, tx),
        out_shape=jax.ShapeDtypeStruct((local, bs, width), f32),
        in_specs=[anywhere, anywhere, scalars, scalars],
        out_specs=anywhere,
        scratch_shapes=[
            pltpu.VMEM((local, bs, width), f32),
            pltpu.VMEM((local, slots, bs, bs), f32),
            pltpu.VMEM((local, bs, slots * bs), f32),
            pltpu.VMEM((local, bs, width), f32),
            pltpu.VMEM((local, bs, width), f32),
            pltpu.VMEM((2, 2, tx, bs, width), f32),
            pltpu.VMEM((2, 2, TY, bs, width), f32),
            dma((2,)),
            dma((local,)),
            dma((2, 2, tx)),
            dma((2, 2, tx)),
            dma((2, 2, TY)),
            dma((2, 2, TY)),
        ],
        compiler_params=pltpu.CompilerParams(
            collective_id=0, has_side_effects=True, vmem_limit_bytes=32 << 20
        ),
        cost_estimate=pl.CostEstimate(
            flops=2 * 2 * local * slots * bs * bs * width, bytes_accessed=5 << 20, transcendentals=0
        ),
        name="filter_steps",
    )(vectors.reshape(local, bs, width), blocks, pattern, counts)
    return result.reshape(local * bs, width)


def solution(mesh):
    placed = (
        P(("row", "col"), None),
        P(("row", "col"), None, None, None),
        P(("row", "col"), None),
        P(("row", "col")),
    )
    return jax.shard_map(
        body, mesh=mesh, in_specs=placed, out_specs=P(("row", "col"), None), check_vma=False
    )
```

```python
import functools

import jax
import jax.numpy as jnp
from jax import lax
from jax.experimental import pallas as pl
from jax.experimental.pallas import tpu as pltpu
from jax.sharding import PartitionSpec as P

TY = 2
GROUP = 8
MESH = pl.DeviceIdType.MESH

center_shift = 0.25
half_range = 1.0


def dot(a, b):
    return jnp.dot(a, b, precision=lax.Precision.HIGHEST, preferred_element_type=jnp.float32)


def kernel(
    rows, cols, tx,
    vec_hbm, blk_hbm, pattern, counts, out_hbm,
    vec, blk, amat, first, out, halo, relay, halo_col, col_relay,
    load_sem, store_sem, near_send, near_recv, far_send, far_recv, pass_send, pass_recv, col_send, col_recv,
    turn_send, turn_recv, near_ready, far_ready,
):
    bs = blk.shape[2]
    width = vec.shape[-1]
    slots = blk.shape[1]
    sites = TY * tx
    me_r, me_c = lax.axis_index("row"), lax.axis_index("col")
    even = 1 - lax.rem(me_r, 2)
    partner = (me_r - 1 + 2 * even, me_c)
    relay_to = (lax.rem(me_r + rows + 2 - 4 * even, rows), me_c)
    relay_from = (lax.rem(me_r + rows - 2 + 4 * even, rows), me_c)
    facing = (even, 1 - even)
    left, right = lax.rem(me_c + cols - 1, cols), lax.rem(me_c + 1, cols)
    place = lax.rem(me_c, GROUP)
    group = me_c - place
    group_before, group_after = lax.rem(group + cols - GROUP, cols), lax.rem(group + GROUP, cols)
    core = lax.rem(me_c, 2)
    inner = (place > 0) & (place < GROUP - 1)

    load_blk = pltpu.make_async_copy(blk_hbm, blk, load_sem.at[0])
    load_vec = pltpu.make_async_copy(vec_hbm, vec, load_sem.at[1])
    load_vec.start()
    load_blk.start()

    barrier = pltpu.get_barrier_semaphore()

    def tell(row, column):
        pl.semaphore_signal(barrier, inc=1, device_id=(row, column), device_id_type=MESH)

    def leader(column):
        return column - lax.rem(column, 2)

    tell(partner[0], leader(me_c))
    tell(me_r, leader(left))

    @pl.when(core == 1)
    def _():
        tell(me_r, leader(right))

    @pl.when(place == 0)
    def _():
        for k in range(3):
            tell(me_r, group_before + 2 * k)

    @pl.when(place == GROUP - 1)
    def _():
        for k in range(3):
            tell(me_r, group_after + 2 * k + 2)

    @pl.when(inner)
    def _():
        tell(me_r, group + (GROUP - 2) * core)

    tell(relay_from[0], leader(me_c) + 1)

    @pl.when(core == 0)
    def _():
        at_end = (place == 0) | (place == GROUP - 2)

        @pl.when(at_end)
        def _():
            pl.semaphore_wait(barrier, 9)

        @pl.when(jnp.logical_not(at_end))
        def _():
            pl.semaphore_wait(barrier, 7)

        pl.semaphore_signal(near_ready, inc=1, device_id=(me_r, me_c + 1), device_id_type=MESH)

    @pl.when(core == 1)
    def _():
        pl.semaphore_wait(near_ready, 1)

    def site(kind, v):
        return facing[kind] * tx + v

    def near_copy(source, step, v):
        return pltpu.make_async_remote_copy(
            src_ref=source.at[site(0, v)], dst_ref=halo.at[step, 0, v],
            send_sem=near_send.at[step, v], recv_sem=near_recv.at[step, v],
            device_id=partner, device_id_type=MESH,
        )

    def far_copy(source, step, v):
        return pltpu.make_async_remote_copy(
            src_ref=source.at[site(1, v)], dst_ref=relay.at[step, v],
            send_sem=far_send.at[step, v], recv_sem=far_recv.at[step, v],
            device_id=relay_to, device_id_type=MESH,
        )

    def pass_copy(step, v):
        return pltpu.make_async_remote_copy(
            src_ref=relay.at[step, v], dst_ref=halo.at[step, 1, v],
            send_sem=pass_send.at[step, v], recv_sem=pass_recv.at[step, v],
            device_id=partner, device_id_type=MESH,
        )

    def col_copy(source, step, side, u):
        v = 0 if side == 0 else tx - 1
        return pltpu.make_async_remote_copy(
            src_ref=source.at[u * tx + v], dst_ref=halo_col.at[step, 1 - side, u],
            send_sem=col_send.at[step, 1 - side, u], recv_sem=col_recv.at[step, 1 - side, u],
            device_id=(me_r, (left, right)[side]), device_id_type=MESH,
        )

    def quarter_copy(source, step, side, u, part):
        a = u * tx + (0 if side == 0 else tx - 1)
        k = 2 * u + part
        if k == 3:
            dst, recv, column = halo_col.at[step, 1 - side, u, part], col_recv.at[step, 1 - side, u], (left, right)[side]
        else:
            dst, recv, column = col_relay.at[step], turn_recv.at[step], group + 2 * k + 2 - side
        return pltpu.make_async_remote_copy(
            src_ref=source.at[a, part], dst_ref=dst,
            send_sem=col_send.at[step, 1 - side, u], recv_sem=recv,
            device_id=(me_r, column), device_id_type=MESH,
        )

    def turn_copy(step):
        k = (place - 1) // 2
        u, part = k // 2, lax.rem(k, 2)
        column = jnp.where(core == 1, group_after, group_before + GROUP - 1)
        return pltpu.make_async_remote_copy(
            src_ref=col_relay.at[step], dst_ref=halo_col.at[step, 1 - core, u, part],
            send_sem=turn_send.at[step], recv_sem=col_recv.at[step, 1 - core, u],
            device_id=(me_r, column), device_id_type=MESH,
        )

    def send_columns(source, step):
        for side in range(2):
            end = (GROUP - 1) * side

            @pl.when(place == end)
            def _():
                for u in range(TY):
                    for part in range(2):
                        quarter_copy(source, step, side, u, part).start()

            @pl.when(place != end)
            def _():
                for u in range(TY):
                    col_copy(source, step, side, u).start()

    def turn(step):
        @pl.when(inner)
        def _():
            pltpu.make_async_copy(col_relay.at[step], col_relay.at[step], turn_recv.at[step]).wait()
            turn_copy(step).start()

    edges = [0, tx - 1]
    inside = list(range(1, tx - 1))
    send_columns(vec_hbm, 0)
    for v in edges:
        near_copy(vec_hbm, 0, v).start()

    def site_id(y, x):
        return ((y // TY * cols + x // tx) * TY + y % TY) * tx + x % tx

    load_blk.wait()
    for u in range(TY):
        for v in range(tx):
            a = u * tx + v
            y, x = me_r * TY + u, me_c * tx + v
            up = lax.rem(y + TY * rows - 1, TY * rows)
            down = lax.rem(y + 1, TY * rows)
            west = lax.rem(x + tx * cols - 1, tx * cols)
            east = lax.rem(x + 1, tx * cols)
            target = [(y, x), (down if u == 0 else up, x), (y, west), (y, east), (up if u == 0 else down, x)]
            for d in range(5):
                name = site_id(*target[d])
                slot = jnp.int32(0)
                for s in range(1, slots):
                    slot = jnp.where(pattern[a, s] == name, s, slot)
                live = jnp.where(slot < counts[a], 1.0, 0.0)
                amat[a, :, d * bs:(d + 1) * bs] = blk[a, slot] * live

    turn(0)

    @pl.when(me_r < 2)
    def _():
        for v in inside:
            near_copy(vec_hbm, 0, v).start()

    @pl.when(core == 1)
    def _():
        pl.semaphore_wait(barrier, 2)
        pl.semaphore_signal(far_ready, inc=1, device_id=(me_r, me_c - 1), device_id_type=MESH)

    @pl.when(core == 0)
    def _():
        pl.semaphore_wait(far_ready, 1)

    for v in edges + inside:
        far_copy(vec_hbm, 0, v).start()
    for v in edges:
        far_copy(vec_hbm, 0, v).wait_recv()
        pass_copy(0, v).start()

    @pl.when(me_r >= 2)
    def _():
        for v in inside:
            near_copy(vec_hbm, 0, v).start()

    for v in inside:
        far_copy(vec_hbm, 0, v).wait_recv()
        pass_copy(0, v).start()
    load_vec.wait()

    def block(ref):
        return ref[...].reshape(bs, width)

    def store(ref, a, value):
        ref[a] = value.reshape(2, bs // 2, width)

    def coupled(a, first_d, *refs):
        field = jnp.concatenate([block(ref) for ref in refs], axis=0)
        return dot(amat[a, :, first_d * bs:(first_d + len(refs)) * bs], field)

    def partial(field, u, v):
        a = u * tx + v
        total = coupled(a, 0, field.at[a], field.at[(1 - u) * tx + v]) - center_shift * block(field.at[a])
        if v == 0:
            return total + coupled(a, 3, field.at[a + 1])
        if v == tx - 1:
            return total + coupled(a, 2, field.at[a - 1])
        return total + coupled(a, 2, field.at[a - 1], field.at[a + 1])

    def from_columns(step, u, v):
        side = 0 if v == 0 else 1
        return coupled(u * tx + v, 2 + side, halo_col.at[step, side, u])

    def from_rows(field, step, kind, v):
        if kind == 0:
            near_copy(field, step, v).wait_recv()
        else:
            pass_copy(step, v).wait_recv()
        return coupled(site(kind, v), 4, halo.at[step, kind, v])

    def wait_columns(field, step):
        for u in range(TY):
            for side in range(2):
                col_copy(field, step, side, u).wait_recv()

    for v in inside + edges:
        for u in range(TY):
            store(first, u * tx + v, partial(vec, u, v))
    wait_columns(vec, 0)
    for v in edges:
        for u in range(TY):
            a = u * tx + v
            store(first, a, block(first.at[a]) + from_columns(0, u, v))
    for some in (edges, inside):
        for kind in range(2):
            for v in some:
                a = site(kind, v)
                store(first, a, (block(first.at[a]) + from_rows(vec, 0, kind, v)) / half_range)
                if kind == 0:
                    near_copy(first, 1, v).start()
                else:
                    far_copy(first, 1, v).start()
        if some is edges:
            send_columns(first, 1)
        for v in some:
            far_copy(first, 1, v).wait_recv()
            pass_copy(1, v).start()
        if some is edges:
            turn(1)

    def finish(a, value):
        store(out, a, 2.0 * (value / half_range) - block(vec.at[a]))
        pltpu.make_async_copy(out.at[a], out_hbm.at[a], store_sem.at[a]).start()

    for v in inside + edges:
        for u in range(TY):
            store(out, u * tx + v, partial(first, u, v))
    for kind in range(2):
        for v in edges:
            a = site(kind, v)
            store(out, a, block(out.at[a]) + from_rows(first, 1, kind, v))
    for v in inside:
        a = site(0, v)
        finish(a, block(out.at[a]) + from_rows(first, 1, 0, v))
    wait_columns(first, 1)
    for v in edges:
        for u in range(TY):
            a = u * tx + v
            finish(a, block(out.at[a]) + from_columns(1, u, v))
    for v in inside:
        a = site(1, v)
        finish(a, block(out.at[a]) + from_rows(first, 1, 1, v))

    for step, field in ((0, vec_hbm), (1, first)):
        for v in range(tx):
            near_copy(field, step, v).wait_send()
            far_copy(field, step, v).wait_send()
            pass_copy(step, v).wait_send()
        for u in range(TY):
            for side in range(2):
                col_copy(field, step, side, u).wait_send()

        @pl.when(inner)
        def _():
            turn_copy(step).wait_send()

    for a in range(sites):
        pltpu.make_async_copy(out.at[a], out_hbm.at[a], store_sem.at[a]).wait()


def body(vectors, blocks, pattern, counts):
    local, slots, bs, _ = blocks.shape
    width = vectors.shape[1]
    rows, cols = lax.axis_size("row"), lax.axis_size("col")
    tx = local // TY
    f32 = jnp.float32
    anywhere = pl.BlockSpec(memory_space=pl.ANY)
    scalars = pl.BlockSpec(memory_space=pltpu.SMEM)
    dma = pltpu.SemaphoreType.DMA
    result = pl.pallas_call(
        functools.partial(kernel, rows, cols, tx),
        out_shape=jax.ShapeDtypeStruct((local, 2, bs // 2, width), f32),
        in_specs=[anywhere, anywhere, scalars, scalars],
        out_specs=anywhere,
        scratch_shapes=[
            pltpu.VMEM((local, 2, bs // 2, width), f32),
            pltpu.VMEM((local, slots, bs, bs), f32),
            pltpu.VMEM((local, bs, slots * bs), f32),
            pltpu.VMEM((local, 2, bs // 2, width), f32),
            pltpu.VMEM((local, 2, bs // 2, width), f32),
            pltpu.VMEM((2, 2, tx, 2, bs // 2, width), f32),
            pltpu.VMEM((2, tx, 2, bs // 2, width), f32),
            pltpu.VMEM((2, 2, TY, 2, bs // 2, width), f32),
            pltpu.VMEM((2, bs // 2, width), f32),
            dma((2,)),
            dma((local,)),
            dma((2, tx)),
            dma((2, tx)),
            dma((2, tx)),
            dma((2, tx)),
            dma((2, tx)),
            dma((2, tx)),
            dma((2, 2, TY)),
            dma((2, 2, TY)),
            dma((2,)),
            dma((2,)),
            pltpu.SemaphoreType.REGULAR,
            pltpu.SemaphoreType.REGULAR,
        ],
        compiler_params=pltpu.CompilerParams(
            collective_id=0, has_side_effects=True, vmem_limit_bytes=60 << 20
        ),
        cost_estimate=pl.CostEstimate(
            flops=2 * 2 * local * slots * bs * bs * width, bytes_accessed=5 << 20, transcendentals=0
        ),
        name="filter_steps",
    )(vectors.reshape(local, 2, bs // 2, width), blocks, pattern, counts)
    return result.reshape(local * bs, width)


def solution(mesh):
    placed = (
        P(("row", "col"), None),
        P(("row", "col"), None, None, None),
        P(("row", "col"), None),
        P(("row", "col")),
    )
    return jax.shard_map(
        body, mesh=mesh, in_specs=placed, out_specs=P(("row", "col"), None), check_vma=False
    )
```

```python
import functools

import jax
import jax.numpy as jnp
from jax import lax
from jax.experimental import pallas as pl
from jax.experimental.pallas import tpu as pltpu
from jax.sharding import PartitionSpec as P

TY = 2
GROUP = 8
MESH = pl.DeviceIdType.MESH

center_shift = 0.25
half_range = 1.0


def dot(a, b):
    return jnp.dot(a, b, precision=lax.Precision.HIGHEST, preferred_element_type=jnp.float32)


def kernel(
    rows, cols, tx,
    vec_hbm, blk_hbm, pattern_hbm, counts_hbm, out,
    pattern, counts, vec, blk, amat, first, halo, relay, halo_col, col_relay,
    load_sem, near_send, near_recv, far_send, far_recv, pass_send, pass_recv, col_send, col_recv,
    turn_send, turn_recv, near_ready, far_ready,
):
    bs = blk.shape[2]
    width = vec.shape[-1]
    slots = blk.shape[1]
    me_r, me_c = lax.axis_index("row"), lax.axis_index("col")
    even = 1 - lax.rem(me_r, 2)
    partner = (me_r - 1 + 2 * even, me_c)
    relay_to = (lax.rem(me_r + rows + 2 - 4 * even, rows), me_c)
    relay_from = (lax.rem(me_r + rows - 2 + 4 * even, rows), me_c)
    facing = (even, 1 - even)
    left, right = lax.rem(me_c + cols - 1, cols), lax.rem(me_c + 1, cols)
    place = lax.rem(me_c, GROUP)
    group = me_c - place
    group_before, group_after = lax.rem(group + cols - GROUP, cols), lax.rem(group + GROUP, cols)
    core = lax.rem(me_c, 2)
    inner = (place > 0) & (place < GROUP - 1)

    load_blk = pltpu.make_async_copy(blk_hbm, blk, load_sem.at[0])
    load_vec = pltpu.make_async_copy(vec_hbm, vec, load_sem.at[1])
    load_pattern = pltpu.make_async_copy(pattern_hbm, pattern, load_sem.at[2])
    load_counts = pltpu.make_async_copy(counts_hbm, counts, load_sem.at[3])

    barrier = pltpu.get_barrier_semaphore()

    def tell(row, column):
        pl.semaphore_signal(barrier, inc=1, device_id=(row, column), device_id_type=MESH)

    def leader(column):
        return column - lax.rem(column, 2)

    tell(partner[0], leader(me_c))

    @pl.when(core == 1)
    def _():
        tell(me_r, me_c - 1)

    @pl.when(core == 0)
    def _():
        tell(me_r, left)

    tell(me_r, leader(right) + 1)
    tell(relay_from[0], leader(me_c) + 1)

    @pl.when(place == 0)
    def _():
        for k in range(3):
            tell(me_r, group_before + 2 * k + 1)

    @pl.when(place == GROUP - 1)
    def _():
        for k in range(3):
            tell(me_r, group_after + 2 * k + 3)

    @pl.when(inner)
    def _():
        tell(me_r, group + 1 + (GROUP - 2) * core)

    load_pattern.start()
    load_counts.start()
    load_vec.start()
    load_blk.start()

    @pl.when(core == 0)
    def _():
        pl.semaphore_wait(barrier, 3)
        pl.semaphore_signal(near_ready, inc=1, device_id=(me_r, me_c + 1), device_id_type=MESH)

    @pl.when(core == 1)
    def _():
        pl.semaphore_wait(near_ready, 1)

    def site(kind, v):
        return facing[kind] * tx + v

    def near_copy(source, step, v):
        return pltpu.make_async_remote_copy(
            src_ref=source.at[site(0, v)], dst_ref=halo.at[step, 0, v],
            send_sem=near_send.at[step, v], recv_sem=near_recv.at[step, v],
            device_id=partner, device_id_type=MESH,
        )

    def far_copy(source, step, v):
        return pltpu.make_async_remote_copy(
            src_ref=source.at[site(1, v)], dst_ref=relay.at[step, v],
            send_sem=far_send.at[step, v], recv_sem=far_recv.at[step, v],
            device_id=relay_to, device_id_type=MESH,
        )

    def pass_copy(step, v):
        return pltpu.make_async_remote_copy(
            src_ref=relay.at[step, v], dst_ref=halo.at[step, 1, v],
            send_sem=pass_send.at[step, v], recv_sem=pass_recv.at[step, v],
            device_id=partner, device_id_type=MESH,
        )

    def col_copy(source, step, side, u):
        v = 0 if side == 0 else tx - 1
        return pltpu.make_async_remote_copy(
            src_ref=source.at[u * tx + v], dst_ref=halo_col.at[step, 1 - side, u],
            send_sem=col_send.at[step, 1 - side, u], recv_sem=col_recv.at[step, 1 - side, u],
            device_id=(me_r, (left, right)[side]), device_id_type=MESH,
        )

    def quarter_copy(source, step, side, u, part):
        a = u * tx + (0 if side == 0 else tx - 1)
        k = 2 * u + part
        if k == 3:
            dst, recv, column = halo_col.at[step, 1 - side, u, part], col_recv.at[step, 1 - side, u], (left, right)[side]
        else:
            dst, recv, column = col_relay.at[step], turn_recv.at[step], group + 2 * k + 2 - side
        return pltpu.make_async_remote_copy(
            src_ref=source.at[a, part], dst_ref=dst,
            send_sem=col_send.at[step, 1 - side, u], recv_sem=recv,
            device_id=(me_r, column), device_id_type=MESH,
        )

    def turn_copy(step):
        k = (place - 1) // 2
        u, part = k // 2, lax.rem(k, 2)
        column = jnp.where(core == 1, group_after, group_before + GROUP - 1)
        return pltpu.make_async_remote_copy(
            src_ref=col_relay.at[step], dst_ref=halo_col.at[step, 1 - core, u, part],
            send_sem=turn_send.at[step], recv_sem=col_recv.at[step, 1 - core, u],
            device_id=(me_r, column), device_id_type=MESH,
        )

    def send_columns(source, step):
        for side in range(2):
            end = (GROUP - 1) * side

            @pl.when(place == end)
            def _():
                for u in range(TY):
                    for part in range(2):
                        quarter_copy(source, step, side, u, part).start()

            @pl.when(place != end)
            def _():
                for u in range(TY):
                    col_copy(source, step, side, u).start()

    def turn(step):
        @pl.when(inner)
        def _():
            pltpu.make_async_copy(col_relay.at[step], col_relay.at[step], turn_recv.at[step]).wait()
            turn_copy(step).start()

    edges = [0, tx - 1]
    inside = list(range(1, tx - 1))
    for v in edges:
        near_copy(vec_hbm, 0, v).start()

    @pl.when(me_r < 2)
    def _():
        for v in inside:
            near_copy(vec_hbm, 0, v).start()

    at_end = (place == 1) | (place == GROUP - 1)

    @pl.when((core == 1) & at_end)
    def _():
        pl.semaphore_wait(barrier, 9)

    @pl.when((core == 1) & jnp.logical_not(at_end))
    def _():
        pl.semaphore_wait(barrier, 7)

    @pl.when(core == 1)
    def _():
        pl.semaphore_signal(far_ready, inc=1, device_id=(me_r, me_c - 1), device_id_type=MESH)

    @pl.when(core == 0)
    def _():
        pl.semaphore_wait(far_ready, 1)

    send_columns(vec_hbm, 0)
    for v in edges + inside:
        far_copy(vec_hbm, 0, v).start()

    def site_id(y, x):
        return ((y // TY * cols + x // tx) * TY + y % TY) * tx + x % tx

    load_pattern.wait()
    load_counts.wait()
    load_blk.wait()
    for u in range(TY):
        for v in range(tx):
            a = u * tx + v
            y, x = me_r * TY + u, me_c * tx + v
            up = lax.rem(y + TY * rows - 1, TY * rows)
            down = lax.rem(y + 1, TY * rows)
            west = lax.rem(x + tx * cols - 1, tx * cols)
            east = lax.rem(x + 1, tx * cols)
            target = [(y, x), (down if u == 0 else up, x), (y, west), (y, east), (up if u == 0 else down, x)]
            for d in range(5):
                name = site_id(*target[d])
                slot = jnp.int32(0)
                for s in range(1, slots):
                    slot = jnp.where(pattern[a, s] == name, s, slot)
                live = jnp.where(slot < counts[a], 1.0, 0.0)
                amat[a, :, d * bs:(d + 1) * bs] = blk[a, slot] * live

    turn(0)
    for v in edges:
        far_copy(vec_hbm, 0, v).wait_recv()
        pass_copy(0, v).start()

    @pl.when(me_r >= 2)
    def _():
        for v in inside:
            near_copy(vec_hbm, 0, v).start()

    for v in inside:
        far_copy(vec_hbm, 0, v).wait_recv()
        pass_copy(0, v).start()
    load_vec.wait()

    def block(ref):
        return ref[...].reshape(bs, width)

    def store(ref, a, value):
        ref[a] = value.reshape(2, bs // 2, width)

    def coupled(a, first_d, *refs):
        field = jnp.concatenate([block(ref) for ref in refs], axis=0)
        return dot(amat[a, :, first_d * bs:(first_d + len(refs)) * bs], field)

    def partial(field, u, v):
        a = u * tx + v
        total = coupled(a, 0, field.at[a], field.at[(1 - u) * tx + v]) - center_shift * block(field.at[a])
        if v == 0:
            return total + coupled(a, 3, field.at[a + 1])
        if v == tx - 1:
            return total + coupled(a, 2, field.at[a - 1])
        return total + coupled(a, 2, field.at[a - 1], field.at[a + 1])

    def from_columns(step, u, v):
        side = 0 if v == 0 else 1
        return coupled(u * tx + v, 2 + side, halo_col.at[step, side, u])

    def from_rows(field, step, kind, v):
        if kind == 0:
            near_copy(field, step, v).wait_recv()
        else:
            pass_copy(step, v).wait_recv()
        return coupled(site(kind, v), 4, halo.at[step, kind, v])

    def wait_columns(field, step):
        for u in range(TY):
            for side in range(2):
                col_copy(field, step, side, u).wait_recv()

    for v in inside + edges:
        for u in range(TY):
            store(first, u * tx + v, partial(vec, u, v))
    wait_columns(vec, 0)
    for v in edges:
        for u in range(TY):
            a = u * tx + v
            store(first, a, block(first.at[a]) + from_columns(0, u, v))

    def first_step(kind, some):
        for v in some:
            a = site(kind, v)
            store(first, a, (block(first.at[a]) + from_rows(vec, 0, kind, v)) / half_range)
            if kind == 0:
                near_copy(first, 1, v).start()
            else:
                far_copy(first, 1, v).start()

    def pass_on(some):
        for v in some:
            far_copy(first, 1, v).wait_recv()
            pass_copy(1, v).start()

    first_step(0, edges)
    first_step(1, edges)
    send_columns(first, 1)
    first_step(0, inside)
    pass_on(edges)
    turn(1)
    first_step(1, inside)
    pass_on(inside)

    def finish(a, value):
        store(out, a, 2.0 * (value / half_range) - block(vec.at[a]))

    for v in inside + edges:
        for u in range(TY):
            store(out, u * tx + v, partial(first, u, v))
    for v in edges:
        a = site(0, v)
        store(out, a, block(out.at[a]) + from_rows(first, 1, 0, v))
    for v in inside:
        a = site(0, v)
        finish(a, block(out.at[a]) + from_rows(first, 1, 0, v))
    for v in edges:
        a = site(1, v)
        store(out, a, block(out.at[a]) + from_rows(first, 1, 1, v))
    wait_columns(first, 1)
    for v in edges:
        for u in range(TY):
            a = u * tx + v
            finish(a, block(out.at[a]) + from_columns(1, u, v))
    for v in inside:
        a = site(1, v)
        finish(a, block(out.at[a]) + from_rows(first, 1, 1, v))

    for step, field in ((0, vec_hbm), (1, first)):
        for v in range(tx):
            near_copy(field, step, v).wait_send()
            far_copy(field, step, v).wait_send()
            pass_copy(step, v).wait_send()
        for u in range(TY):
            for side in range(2):
                col_copy(field, step, side, u).wait_send()

        @pl.when(inner)
        def _():
            turn_copy(step).wait_send()


def body(vectors, blocks, pattern, counts):
    local, slots, bs, _ = blocks.shape
    width = vectors.shape[1]
    rows, cols = lax.axis_size("row"), lax.axis_size("col")
    tx = local // TY
    f32 = jnp.float32
    stays = pl.BlockSpec(memory_space=pltpu.HBM)
    operands = [
        pltpu.with_memory_space_constraint(operand, pltpu.HBM)
        for operand in (vectors.reshape(local, 2, bs // 2, width), blocks, pattern, counts)
    ]
    dma = pltpu.SemaphoreType.DMA
    result = pl.pallas_call(
        functools.partial(kernel, rows, cols, tx),
        out_shape=jax.ShapeDtypeStruct((local, 2, bs // 2, width), f32),
        in_specs=[stays] * 4,
        out_specs=pl.BlockSpec(memory_space=pltpu.VMEM),
        scratch_shapes=[
            pltpu.SMEM(pattern.shape, jnp.int32),
            pltpu.SMEM(counts.shape, jnp.int32),
            pltpu.VMEM((local, 2, bs // 2, width), f32),
            pltpu.VMEM((local, slots, bs, bs), f32),
            pltpu.VMEM((local, bs, slots * bs), f32),
            pltpu.VMEM((local, 2, bs // 2, width), f32),
            pltpu.VMEM((2, 2, tx, 2, bs // 2, width), f32),
            pltpu.VMEM((2, tx, 2, bs // 2, width), f32),
            pltpu.VMEM((2, 2, TY, 2, bs // 2, width), f32),
            pltpu.VMEM((2, bs // 2, width), f32),
            dma((4,)),
            dma((2, tx)),
            dma((2, tx)),
            dma((2, tx)),
            dma((2, tx)),
            dma((2, tx)),
            dma((2, tx)),
            dma((2, 2, TY)),
            dma((2, 2, TY)),
            dma((2,)),
            dma((2,)),
            pltpu.SemaphoreType.REGULAR,
            pltpu.SemaphoreType.REGULAR,
        ],
        compiler_params=pltpu.CompilerParams(
            collective_id=0, has_side_effects=True, vmem_limit_bytes=24 << 20
        ),
        cost_estimate=pl.CostEstimate(
            flops=2 * 2 * local * slots * bs * bs * width, bytes_accessed=5 << 20, transcendentals=0
        ),
        name="filter_steps",
    )(*operands)
    return result.reshape(local * bs, width)


def solution(mesh):
    placed = (
        P(("row", "col"), None),
        P(("row", "col"), None, None, None),
        P(("row", "col"), None),
        P(("row", "col")),
    )
    return jax.shard_map(
        body, mesh=mesh, in_specs=placed, out_specs=P(("row", "col"), None), check_vma=False
    )
```

```python
import functools

import jax
import jax.numpy as jnp
from jax import lax
from jax.experimental import pallas as pl
from jax.experimental.pallas import tpu as pltpu
from jax.sharding import PartitionSpec as P

TY = 2
GROUP = 8
MESH = pl.DeviceIdType.MESH

center_shift = 0.25
half_range = 1.0


def dot(a, b):
    return jnp.dot(a, b, precision=lax.Precision.HIGHEST, preferred_element_type=jnp.float32)


def kernel(
    rows, cols, tx,
    vec_hbm, blk_hbm, pattern_hbm, counts_hbm, out,
    pattern, counts, vec, blk, amat, first, halo, relay, halo_col, col_relay,
    load_sem, near_send, near_recv, far_send, far_recv, pass_send, pass_recv, col_send, col_recv,
    turn_send, turn_recv, rest_ready,
):
    bs = blk.shape[2]
    width = vec.shape[-1]
    slots = blk.shape[1]
    me_r, me_c = lax.axis_index("row"), lax.axis_index("col")
    even = 1 - lax.rem(me_r, 2)
    partner = (me_r - 1 + 2 * even, me_c)
    relay_to = (lax.rem(me_r + rows + 2 - 4 * even, rows), me_c)
    relay_from = (lax.rem(me_r + rows - 2 + 4 * even, rows), me_c)
    facing = (even, 1 - even)
    left, right = lax.rem(me_c + cols - 1, cols), lax.rem(me_c + 1, cols)
    place = lax.rem(me_c, GROUP)
    group = me_c - place
    group_before, group_after = lax.rem(group + cols - GROUP, cols), lax.rem(group + GROUP, cols)
    core = lax.rem(me_c, 2)
    inner = (place > 0) & (place < GROUP - 1)

    load_blk = pltpu.make_async_copy(blk_hbm, blk, load_sem.at[0])
    load_vec = pltpu.make_async_copy(vec_hbm, vec, load_sem.at[1])
    load_pattern = pltpu.make_async_copy(pattern_hbm, pattern, load_sem.at[2])
    load_counts = pltpu.make_async_copy(counts_hbm, counts, load_sem.at[3])

    barrier = pltpu.get_barrier_semaphore()

    def tell(row, column):
        pl.semaphore_signal(barrier, inc=1, device_id=(row, column), device_id_type=MESH)

    def leader(column):
        return column - lax.rem(column, 2)

    tell(*partner)
    tell(me_r, leader(left))
    tell(relay_from[0], leader(me_c))

    @pl.when(core == 1)
    def _():
        tell(me_r, right)

    @pl.when(place == 0)
    def _():
        for k in range(3):
            tell(me_r, group_before + 2 * k)

    @pl.when(place == GROUP - 1)
    def _():
        for k in range(3):
            tell(me_r, group_after + 2 * k + 2)

    @pl.when(inner)
    def _():
        tell(me_r, group + (GROUP - 2) * core)

    load_pattern.start()
    load_counts.start()
    load_vec.start()
    load_blk.start()

    def site(kind, v):
        return facing[kind] * tx + v

    def near_copy(source, step, v):
        return pltpu.make_async_remote_copy(
            src_ref=source.at[site(0, v)], dst_ref=halo.at[step, 0, v],
            send_sem=near_send.at[step, v], recv_sem=near_recv.at[step, v],
            device_id=partner, device_id_type=MESH,
        )

    def far_copy(source, step, v):
        return pltpu.make_async_remote_copy(
            src_ref=source.at[site(1, v)], dst_ref=relay.at[step, v],
            send_sem=far_send.at[step, v], recv_sem=far_recv.at[step, v],
            device_id=relay_to, device_id_type=MESH,
        )

    def pass_copy(step, v):
        return pltpu.make_async_remote_copy(
            src_ref=relay.at[step, v], dst_ref=halo.at[step, 1, v],
            send_sem=pass_send.at[step, v], recv_sem=pass_recv.at[step, v],
            device_id=partner, device_id_type=MESH,
        )

    def col_copy(source, step, side, u):
        v = 0 if side == 0 else tx - 1
        return pltpu.make_async_remote_copy(
            src_ref=source.at[u * tx + v], dst_ref=halo_col.at[step, 1 - side, u],
            send_sem=col_send.at[step, 1 - side, u], recv_sem=col_recv.at[step, 1 - side, u],
            device_id=(me_r, (left, right)[side]), device_id_type=MESH,
        )

    def quarter_copy(source, step, side, u, part):
        a = u * tx + (0 if side == 0 else tx - 1)
        k = 2 * u + part
        if k == 3:
            dst, recv, column = halo_col.at[step, 1 - side, u, part], col_recv.at[step, 1 - side, u], (left, right)[side]
        else:
            dst, recv, column = col_relay.at[step], turn_recv.at[step], group + 2 * k + 2 - side
        return pltpu.make_async_remote_copy(
            src_ref=source.at[a, part], dst_ref=dst,
            send_sem=col_send.at[step, 1 - side, u], recv_sem=recv,
            device_id=(me_r, column), device_id_type=MESH,
        )

    def turn_copy(step):
        k = (place - 1) // 2
        u, part = k // 2, lax.rem(k, 2)
        column = jnp.where(core == 1, group_after, group_before + GROUP - 1)
        return pltpu.make_async_remote_copy(
            src_ref=col_relay.at[step], dst_ref=halo_col.at[step, 1 - core, u, part],
            send_sem=turn_send.at[step], recv_sem=col_recv.at[step, 1 - core, u],
            device_id=(me_r, column), device_id_type=MESH,
        )

    def send_columns(source, step):
        for side in range(2):
            end = (GROUP - 1) * side

            @pl.when(place == end)
            def _():
                for u in range(TY):
                    for part in range(2):
                        quarter_copy(source, step, side, u, part).start()

            @pl.when(place != end)
            def _():
                for u in range(TY):
                    col_copy(source, step, side, u).start()

    def turn(step):
        @pl.when(inner)
        def _():
            pltpu.make_async_copy(col_relay.at[step], col_relay.at[step], turn_recv.at[step]).wait()
            turn_copy(step).start()

    edges = [0, tx - 1]
    inside = list(range(1, tx - 1))
    def forward():
        for v in edges + inside:
            far_copy(vec_hbm, 0, v).wait_recv()
            pass_copy(0, v).start()

    def start_near():
        for v in edges + inside:
            near_copy(vec_hbm, 0, v).start()

    early = (me_r == 0) & (core == 1)
    at_end = (place == 0) | (place == GROUP - 2)

    @pl.when((core == 0) & at_end)
    def _():
        pl.semaphore_wait(barrier, 10)

    @pl.when((core == 0) & jnp.logical_not(at_end))
    def _():
        pl.semaphore_wait(barrier, 8)

    @pl.when(core == 0)
    def _():
        pl.semaphore_signal(rest_ready, inc=1, device_id=(me_r, me_c + 1), device_id_type=MESH)
        start_near()

    @pl.when(core == 1)
    def _():
        pl.semaphore_wait(barrier, 1)
        start_near()

    @pl.when(early)
    def _():
        forward()

    @pl.when(core == 1)
    def _():
        pl.semaphore_wait(rest_ready, 1)

    send_columns(vec_hbm, 0)
    for v in edges + inside:
        far_copy(vec_hbm, 0, v).start()

    def site_id(y, x):
        return ((y // TY * cols + x // tx) * TY + y % TY) * tx + x % tx

    load_pattern.wait()
    load_counts.wait()
    load_blk.wait()
    for u in range(TY):
        for v in range(tx):
            a = u * tx + v
            y, x = me_r * TY + u, me_c * tx + v
            up = lax.rem(y + TY * rows - 1, TY * rows)
            down = lax.rem(y + 1, TY * rows)
            west = lax.rem(x + tx * cols - 1, tx * cols)
            east = lax.rem(x + 1, tx * cols)
            target = [(y, x), (down if u == 0 else up, x), (y, west), (y, east), (up if u == 0 else down, x)]
            for d in range(5):
                name = site_id(*target[d])
                slot = jnp.int32(0)
                for s in range(1, slots):
                    slot = jnp.where(pattern[a, s] == name, s, slot)
                live = jnp.where(slot < counts[a], 1.0, 0.0)
                amat[a, :, d * bs:(d + 1) * bs] = blk[a, slot] * live

    turn(0)

    @pl.when(jnp.logical_not(early))
    def _():
        forward()

    load_vec.wait()

    def block(ref):
        return ref[...].reshape(bs, width)

    def store(ref, a, value):
        ref[a] = value.reshape(2, bs // 2, width)

    def coupled(a, first_d, *refs):
        field = jnp.concatenate([block(ref) for ref in refs], axis=0)
        return dot(amat[a, :, first_d * bs:(first_d + len(refs)) * bs], field)

    def partial(field, u, v):
        a = u * tx + v
        total = coupled(a, 0, field.at[a], field.at[(1 - u) * tx + v]) - center_shift * block(field.at[a])
        if v == 0:
            return total + coupled(a, 3, field.at[a + 1])
        if v == tx - 1:
            return total + coupled(a, 2, field.at[a - 1])
        return total + coupled(a, 2, field.at[a - 1], field.at[a + 1])

    def from_columns(step, u, v):
        side = 0 if v == 0 else 1
        return coupled(u * tx + v, 2 + side, halo_col.at[step, side, u])

    def from_rows(field, step, kind, v):
        if kind == 0:
            near_copy(field, step, v).wait_recv()
        else:
            pass_copy(step, v).wait_recv()
        return coupled(site(kind, v), 4, halo.at[step, kind, v])

    def wait_columns(field, step):
        for u in range(TY):
            for side in range(2):
                col_copy(field, step, side, u).wait_recv()

    for v in inside + edges:
        for u in range(TY):
            store(first, u * tx + v, partial(vec, u, v))
    wait_columns(vec, 0)
    for v in edges:
        for u in range(TY):
            a = u * tx + v
            store(first, a, block(first.at[a]) + from_columns(0, u, v))

    def first_step(kind, some):
        for v in some:
            a = site(kind, v)
            store(first, a, (block(first.at[a]) + from_rows(vec, 0, kind, v)) / half_range)
            if kind == 0:
                near_copy(first, 1, v).start()
            else:
                far_copy(first, 1, v).start()

    def pass_on(some):
        for v in some:
            far_copy(first, 1, v).wait_recv()
            pass_copy(1, v).start()

    first_step(0, edges)
    first_step(1, edges)
    send_columns(first, 1)
    first_step(0, inside)
    turn(1)
    pass_on(edges)
    first_step(1, inside)
    pass_on(inside)

    def finish(a, value):
        store(out, a, 2.0 * (value / half_range) - block(vec.at[a]))

    for v in inside + edges:
        for u in range(TY):
            store(out, u * tx + v, partial(first, u, v))
    for v in edges:
        a = site(0, v)
        store(out, a, block(out.at[a]) + from_rows(first, 1, 0, v))
    for v in inside:
        a = site(0, v)
        finish(a, block(out.at[a]) + from_rows(first, 1, 0, v))
    for v in edges:
        a = site(1, v)
        store(out, a, block(out.at[a]) + from_rows(first, 1, 1, v))
    wait_columns(first, 1)
    for v in edges:
        for u in range(TY):
            a = u * tx + v
            finish(a, block(out.at[a]) + from_columns(1, u, v))
    for v in inside:
        a = site(1, v)
        finish(a, block(out.at[a]) + from_rows(first, 1, 1, v))

    for step, field in ((0, vec_hbm), (1, first)):
        for v in range(tx):
            near_copy(field, step, v).wait_send()
            far_copy(field, step, v).wait_send()
            pass_copy(step, v).wait_send()
        for u in range(TY):
            for side in range(2):
                col_copy(field, step, side, u).wait_send()

        @pl.when(inner)
        def _():
            turn_copy(step).wait_send()


def body(vectors, blocks, pattern, counts):
    local, slots, bs, _ = blocks.shape
    width = vectors.shape[1]
    rows, cols = lax.axis_size("row"), lax.axis_size("col")
    tx = local // TY
    f32 = jnp.float32
    stays = pl.BlockSpec(memory_space=pltpu.HBM)
    operands = [
        pltpu.with_memory_space_constraint(operand, pltpu.HBM)
        for operand in (vectors.reshape(local, 2, bs // 2, width), blocks, pattern, counts)
    ]
    dma = pltpu.SemaphoreType.DMA
    result = pl.pallas_call(
        functools.partial(kernel, rows, cols, tx),
        out_shape=jax.ShapeDtypeStruct((local, 2, bs // 2, width), f32),
        in_specs=[stays] * 4,
        out_specs=pl.BlockSpec(memory_space=pltpu.VMEM),
        scratch_shapes=[
            pltpu.SMEM(pattern.shape, jnp.int32),
            pltpu.SMEM(counts.shape, jnp.int32),
            pltpu.VMEM((local, 2, bs // 2, width), f32),
            pltpu.VMEM((local, slots, bs, bs), f32),
            pltpu.VMEM((local, bs, slots * bs), f32),
            pltpu.VMEM((local, 2, bs // 2, width), f32),
            pltpu.VMEM((2, 2, tx, 2, bs // 2, width), f32),
            pltpu.VMEM((2, tx, 2, bs // 2, width), f32),
            pltpu.VMEM((2, 2, TY, 2, bs // 2, width), f32),
            pltpu.VMEM((2, bs // 2, width), f32),
            dma((4,)),
            dma((2, tx)),
            dma((2, tx)),
            dma((2, tx)),
            dma((2, tx)),
            dma((2, tx)),
            dma((2, tx)),
            dma((2, 2, TY)),
            dma((2, 2, TY)),
            dma((2,)),
            dma((2,)),
            pltpu.SemaphoreType.REGULAR,
        ],
        compiler_params=pltpu.CompilerParams(
            collective_id=0, has_side_effects=True, vmem_limit_bytes=24 << 20
        ),
        cost_estimate=pl.CostEstimate(
            flops=2 * 2 * local * slots * bs * bs * width, bytes_accessed=5 << 20, transcendentals=0
        ),
        name="filter_steps",
    )(*operands)
    return result.reshape(local * bs, width)


def solution(mesh):
    placed = (
        P(("row", "col"), None),
        P(("row", "col"), None, None, None),
        P(("row", "col"), None),
        P(("row", "col")),
    )
    return jax.shard_map(
        body, mesh=mesh, in_specs=placed, out_specs=P(("row", "col"), None), check_vma=False
    )
```

```python
import functools

import jax
import jax.numpy as jnp
from jax import lax
from jax.experimental import pallas as pl
from jax.experimental.pallas import tpu as pltpu
from jax.sharding import PartitionSpec as P

TY = 2
GROUP = 8
MESH = pl.DeviceIdType.MESH

center_shift = 0.25
half_range = 1.0


def dot(a, b):
    return jnp.dot(a, b, precision=lax.Precision.HIGHEST, preferred_element_type=jnp.float32)


def kernel(
    rows, cols, tx,
    vec_hbm, blk_hbm, pattern_hbm, counts_hbm, out,
    pattern, counts, vec, blk, amat, first, halo, relay, halo_col, col_relay,
    load_sem, near_send, near_recv, far_send, far_recv, pass_send, pass_recv, col_send, col_recv,
    turn_send, turn_recv, rest_ready,
):
    bs = blk.shape[2]
    width = vec.shape[-1]
    slots = blk.shape[1]
    me_r, me_c = lax.axis_index("row"), lax.axis_index("col")
    even = 1 - lax.rem(me_r, 2)
    partner = (me_r - 1 + 2 * even, me_c)
    relay_to = (lax.rem(me_r + rows + 2 - 4 * even, rows), me_c)
    relay_from = (lax.rem(me_r + rows - 2 + 4 * even, rows), me_c)
    facing = (even, 1 - even)
    left, right = lax.rem(me_c + cols - 1, cols), lax.rem(me_c + 1, cols)
    place = lax.rem(me_c, GROUP)
    group = me_c - place
    group_before, group_after = lax.rem(group + cols - GROUP, cols), lax.rem(group + GROUP, cols)
    core = lax.rem(me_c, 2)
    inner = (place > 0) & (place < GROUP - 1)

    load_blk = pltpu.make_async_copy(blk_hbm, blk, load_sem.at[0])
    load_vec = pltpu.make_async_copy(vec_hbm, vec, load_sem.at[1])
    load_pattern = pltpu.make_async_copy(pattern_hbm, pattern, load_sem.at[2])
    load_counts = pltpu.make_async_copy(counts_hbm, counts, load_sem.at[3])

    barrier = pltpu.get_barrier_semaphore()

    def tell(row, column):
        pl.semaphore_signal(barrier, inc=1, device_id=(row, column), device_id_type=MESH)

    def leader(column):
        return column - lax.rem(column, 2)

    tell(*partner)
    tell(me_r, leader(left))
    tell(relay_from[0], leader(me_c))

    @pl.when(core == 1)
    def _():
        tell(me_r, right)

    @pl.when(place == 0)
    def _():
        for k in range(3):
            tell(me_r, group_before + 2 * k)

    @pl.when(place == GROUP - 1)
    def _():
        for k in range(3):
            tell(me_r, group_after + 2 * k + 2)

    @pl.when(inner)
    def _():
        tell(me_r, group + (GROUP - 2) * core)

    load_pattern.start()
    load_counts.start()
    load_vec.start()
    load_blk.start()

    def site(kind, v):
        return facing[kind] * tx + v

    def near_copy(source, step, v):
        return pltpu.make_async_remote_copy(
            src_ref=source.at[site(0, v)], dst_ref=halo.at[step, 0, v],
            send_sem=near_send.at[step, v], recv_sem=near_recv.at[step, v],
            device_id=partner, device_id_type=MESH,
        )

    def far_copy(source, step, v):
        return pltpu.make_async_remote_copy(
            src_ref=source.at[site(1, v)], dst_ref=relay.at[step, v],
            send_sem=far_send.at[step, v], recv_sem=far_recv.at[step, v],
            device_id=relay_to, device_id_type=MESH,
        )

    def pass_copy(step, v):
        return pltpu.make_async_remote_copy(
            src_ref=relay.at[step, v], dst_ref=halo.at[step, 1, v],
            send_sem=pass_send.at[step, v], recv_sem=pass_recv.at[step, v],
            device_id=partner, device_id_type=MESH,
        )

    def col_copy(source, step, side, u):
        v = 0 if side == 0 else tx - 1
        return pltpu.make_async_remote_copy(
            src_ref=source.at[u * tx + v], dst_ref=halo_col.at[step, 1 - side, u],
            send_sem=col_send.at[step, 1 - side, u], recv_sem=col_recv.at[step, 1 - side, u],
            device_id=(me_r, (left, right)[side]), device_id_type=MESH,
        )

    def quarter_copy(source, step, side, u, part):
        a = u * tx + (0 if side == 0 else tx - 1)
        k = 2 * u + part
        if k == 3:
            dst, recv, column = halo_col.at[step, 1 - side, u, part], col_recv.at[step, 1 - side, u], (left, right)[side]
        else:
            dst, recv, column = col_relay.at[step], turn_recv.at[step], group + 2 * k + 2 - side
        return pltpu.make_async_remote_copy(
            src_ref=source.at[a, part], dst_ref=dst,
            send_sem=col_send.at[step, 1 - side, u], recv_sem=recv,
            device_id=(me_r, column), device_id_type=MESH,
        )

    def turn_copy(step):
        k = (place - 1) // 2
        u, part = k // 2, lax.rem(k, 2)
        column = jnp.where(core == 1, group_after, group_before + GROUP - 1)
        return pltpu.make_async_remote_copy(
            src_ref=col_relay.at[step], dst_ref=halo_col.at[step, 1 - core, u, part],
            send_sem=turn_send.at[step], recv_sem=col_recv.at[step, 1 - core, u],
            device_id=(me_r, column), device_id_type=MESH,
        )

    def send_columns(source, step):
        for side in range(2):
            end = (GROUP - 1) * side

            @pl.when(place == end)
            def _():
                for u in range(TY):
                    for part in range(2):
                        quarter_copy(source, step, side, u, part).start()

            @pl.when(place != end)
            def _():
                for u in range(TY):
                    col_copy(source, step, side, u).start()

    def turn(step):
        @pl.when(inner)
        def _():
            pltpu.make_async_copy(col_relay.at[step], col_relay.at[step], turn_recv.at[step]).wait()
            turn_copy(step).start()

    edges = [0, tx - 1]
    inside = list(range(1, tx - 1))
    def forward():
        for v in edges + inside:
            far_copy(vec, 0, v).wait_recv()
            pass_copy(0, v).start()

    def start_near():
        for v in edges + inside:
            near_copy(vec, 0, v).start()

    load_vec.wait()

    early = (me_r == 0) & (core == 1)
    at_end = (place == 0) | (place == GROUP - 2)

    @pl.when((core == 0) & at_end)
    def _():
        pl.semaphore_wait(barrier, 10)

    @pl.when((core == 0) & jnp.logical_not(at_end))
    def _():
        pl.semaphore_wait(barrier, 8)

    @pl.when(core == 0)
    def _():
        pl.semaphore_signal(rest_ready, inc=1, device_id=(me_r, me_c + 1), device_id_type=MESH)
        start_near()

    @pl.when(core == 1)
    def _():
        pl.semaphore_wait(barrier, 1)
        start_near()

    @pl.when(early)
    def _():
        forward()

    @pl.when(core == 1)
    def _():
        pl.semaphore_wait(rest_ready, 1)

    send_columns(vec, 0)
    for v in edges + inside:
        far_copy(vec, 0, v).start()

    def site_id(y, x):
        return ((y // TY * cols + x // tx) * TY + y % TY) * tx + x % tx

    load_pattern.wait()
    load_counts.wait()
    load_blk.wait()
    for u in range(TY):
        for v in range(tx):
            a = u * tx + v
            y, x = me_r * TY + u, me_c * tx + v
            up = lax.rem(y + TY * rows - 1, TY * rows)
            down = lax.rem(y + 1, TY * rows)
            west = lax.rem(x + tx * cols - 1, tx * cols)
            east = lax.rem(x + 1, tx * cols)
            target = [(y, x), (down if u == 0 else up, x), (y, west), (y, east), (up if u == 0 else down, x)]
            for d in range(5):
                name = site_id(*target[d])
                slot = jnp.int32(0)
                for s in range(1, slots):
                    slot = jnp.where(pattern[a, s] == name, s, slot)
                live = jnp.where(slot < counts[a], 1.0, 0.0)
                amat[a, :, d * bs:(d + 1) * bs] = blk[a, slot] * live

    turn(0)

    @pl.when(jnp.logical_not(early))
    def _():
        forward()


    def block(ref):
        return ref[...].reshape(bs, width)

    def store(ref, a, value):
        ref[a] = value.reshape(2, bs // 2, width)

    def coupled(a, first_d, *refs):
        field = jnp.concatenate([block(ref) for ref in refs], axis=0)
        return dot(amat[a, :, first_d * bs:(first_d + len(refs)) * bs], field)

    def partial(field, u, v):
        a = u * tx + v
        total = coupled(a, 0, field.at[a], field.at[(1 - u) * tx + v]) - center_shift * block(field.at[a])
        if v == 0:
            return total + coupled(a, 3, field.at[a + 1])
        if v == tx - 1:
            return total + coupled(a, 2, field.at[a - 1])
        return total + coupled(a, 2, field.at[a - 1], field.at[a + 1])

    def from_columns(step, u, v):
        side = 0 if v == 0 else 1
        return coupled(u * tx + v, 2 + side, halo_col.at[step, side, u])

    def from_rows(field, step, kind, v):
        if kind == 0:
            near_copy(field, step, v).wait_recv()
        else:
            pass_copy(step, v).wait_recv()
        return coupled(site(kind, v), 4, halo.at[step, kind, v])

    def wait_columns(field, step):
        for u in range(TY):
            for side in range(2):
                col_copy(field, step, side, u).wait_recv()

    for v in inside + edges:
        for u in range(TY):
            store(first, u * tx + v, partial(vec, u, v))
    wait_columns(vec, 0)
    for v in edges:
        for u in range(TY):
            a = u * tx + v
            store(first, a, block(first.at[a]) + from_columns(0, u, v))

    def first_step(kind, some):
        for v in some:
            a = site(kind, v)
            store(first, a, (block(first.at[a]) + from_rows(vec, 0, kind, v)) / half_range)
            if kind == 0:
                near_copy(first, 1, v).start()
            else:
                far_copy(first, 1, v).start()

    def pass_on(some):
        for v in some:
            far_copy(first, 1, v).wait_recv()
            pass_copy(1, v).start()

    first_step(0, edges)
    first_step(1, edges)
    send_columns(first, 1)
    first_step(0, inside)
    turn(1)
    pass_on(edges)
    first_step(1, inside)
    pass_on(inside)

    def finish(a, value):
        store(out, a, 2.0 * (value / half_range) - block(vec.at[a]))

    for v in inside + edges:
        for u in range(TY):
            store(out, u * tx + v, partial(first, u, v))
    for v in edges:
        a = site(0, v)
        store(out, a, block(out.at[a]) + from_rows(first, 1, 0, v))
    for v in inside:
        a = site(0, v)
        finish(a, block(out.at[a]) + from_rows(first, 1, 0, v))
    for v in edges:
        a = site(1, v)
        store(out, a, block(out.at[a]) + from_rows(first, 1, 1, v))
    wait_columns(first, 1)
    for v in edges:
        for u in range(TY):
            a = u * tx + v
            finish(a, block(out.at[a]) + from_columns(1, u, v))
    for v in inside:
        a = site(1, v)
        finish(a, block(out.at[a]) + from_rows(first, 1, 1, v))

    for step, field in ((0, vec_hbm), (1, first)):
        for v in range(tx):
            near_copy(field, step, v).wait_send()
            far_copy(field, step, v).wait_send()
            pass_copy(step, v).wait_send()
        for u in range(TY):
            for side in range(2):
                col_copy(field, step, side, u).wait_send()

        @pl.when(inner)
        def _():
            turn_copy(step).wait_send()


def body(vectors, blocks, pattern, counts):
    local, slots, bs, _ = blocks.shape
    width = vectors.shape[1]
    rows, cols = lax.axis_size("row"), lax.axis_size("col")
    tx = local // TY
    f32 = jnp.float32
    stays = pl.BlockSpec(memory_space=pltpu.HBM)
    operands = [
        pltpu.with_memory_space_constraint(operand, pltpu.HBM)
        for operand in (vectors.reshape(local, 2, bs // 2, width), blocks, pattern, counts)
    ]
    dma = pltpu.SemaphoreType.DMA
    result = pl.pallas_call(
        functools.partial(kernel, rows, cols, tx),
        out_shape=jax.ShapeDtypeStruct((local, 2, bs // 2, width), f32),
        in_specs=[stays] * 4,
        out_specs=pl.BlockSpec(memory_space=pltpu.VMEM),
        scratch_shapes=[
            pltpu.SMEM(pattern.shape, jnp.int32),
            pltpu.SMEM(counts.shape, jnp.int32),
            pltpu.VMEM((local, 2, bs // 2, width), f32),
            pltpu.VMEM((local, slots, bs, bs), f32),
            pltpu.VMEM((local, bs, slots * bs), f32),
            pltpu.VMEM((local, 2, bs // 2, width), f32),
            pltpu.VMEM((2, 2, tx, 2, bs // 2, width), f32),
            pltpu.VMEM((2, tx, 2, bs // 2, width), f32),
            pltpu.VMEM((2, 2, TY, 2, bs // 2, width), f32),
            pltpu.VMEM((2, bs // 2, width), f32),
            dma((4,)),
            dma((2, tx)),
            dma((2, tx)),
            dma((2, tx)),
            dma((2, tx)),
            dma((2, tx)),
            dma((2, tx)),
            dma((2, 2, TY)),
            dma((2, 2, TY)),
            dma((2,)),
            dma((2,)),
            pltpu.SemaphoreType.REGULAR,
        ],
        compiler_params=pltpu.CompilerParams(
            collective_id=0, has_side_effects=True, vmem_limit_bytes=24 << 20
        ),
        cost_estimate=pl.CostEstimate(
            flops=2 * 2 * local * slots * bs * bs * width, bytes_accessed=5 << 20, transcendentals=0
        ),
        name="filter_steps",
    )(*operands)
    return result.reshape(local * bs, width)


def solution(mesh):
    placed = (
        P(("row", "col"), None),
        P(("row", "col"), None, None, None),
        P(("row", "col"), None),
        P(("row", "col")),
    )
    return jax.shard_map(
        body, mesh=mesh, in_specs=placed, out_specs=P(("row", "col"), None), check_vma=False
    )
```
